256 devices in a mesh: samp: 16 (over y_hi, x, core), par: 16 (over z, y_lo).
Axes of the slice: x: 4, y: 4 (y_hi: 2, y_lo: 2; y = y_hi * 2 + y_lo), z: 8, core: 2. Of those that a mesh axis runs over, the one named last changes fastest.
Arguments:
- log_derivs: float32 [2, 8192, 6144], P(None, 'samp', 'par'), may hold values from -60 to 60, as said below
Outputs:
- gram: float32 [8192, 8192], P('samp', 'par')
The draws below stay inside these ranges and needn't reach their ends.
Inputs may be any that keep to these rules, and one draw needn't show every extreme that they name: `log_derivs`: finite log-derivatives.
All inputs are finite; a program needn't handle non-finite values.
Results may differ from the reference program's by a relative error of at most 0.0001.
Values sent between devices are 32-bit elements; how exact they have to be, the bound alone decides.
A program may use at most 128 MiB of HBM per device.

```python
import jax
import jax.numpy as jnp
from jax import lax

STEPS = 2
SAMPLES = 8192
PARAMS = 6144


def draw_log_derivs(key, part):
    key = jax.random.fold_in(key, 7)
    key_mu, key_col, key_row, key_noise = jax.random.split(key, 4)
    offsets = jax.random.uniform(key_mu, (STEPS, 1, PARAMS), jnp.float32, -1.0, 1.0)
    drift = 1.0 + 2.0 * jnp.arange(SAMPLES, dtype=jnp.float32)[None, :, None] / SAMPLES
    col_scale = jnp.exp(jax.random.uniform(key_col, (STEPS, 1, PARAMS), jnp.float32, jnp.log(0.3), jnp.log(3.0)))
    row_scale = jnp.exp(jax.random.uniform(key_row, (1, SAMPLES, 1), jnp.float32, jnp.log(0.4), jnp.log(2.0)))
    noise = jnp.clip(jax.random.normal(key_noise, (STEPS, SAMPLES, PARAMS), jnp.float32), -6.0, 6.0)
    return offsets * drift + col_scale * row_scale * noise


def setup_inputs(seed: int = 0) -> dict:
    seeds = jax.random.split(jax.random.key(seed), 2)
    log_derivs = draw_log_derivs(jax.random.fold_in(seeds[1], 71), 0)
    return {"log_derivs": log_derivs}


def reference(log_derivs):
    col_mean = jnp.mean(log_derivs, axis=1)
    centered = log_derivs - col_mean[:, None, :]
    gram_sum = jnp.zeros((SAMPLES, SAMPLES), jnp.float32)
    for slab_index in range(STEPS):
        slab = centered[slab_index]
        gram_sum = gram_sum + jnp.dot(slab, slab.T, precision=lax.Precision.HIGHEST, preferred_element_type=jnp.float32)
    return gram_sum / (STEPS * PARAMS)
```

```python
import functools

import jax
import jax.numpy as jnp
from jax import lax
from jax.experimental import pallas as pl
from jax.experimental.pallas import tpu as pltpu
from jax.sharding import PartitionSpec as P

MESH = pl.DeviceIdType.MESH
NX, NY, NZ = 4, 4, 8
UNIT = 512
HALF = UNIT // 2
PART = 384
KU = 2 * PART
N = 4
CH = HALF // N
SAMPLES = 8192
SCALE = 1.0 / 12288.0

ONCE = ["sib0", "sib1", "m1a", "m1b", "m1c", "m2a", "m2b", "m2c", "row0", "row1"]
EACH = [
    "oa", "ob", "j0", "xr", "xl", "fr", "fl", "j1", "j2", "j3", "g0", "g1", "g2", "g3",
    "z0p", "z0m", "z1p", "z1m", "z2p", "z2m", "z3p", "z3m", "fin",
]
SEMS = len(ONCE) + N * len(EACH)


def slot(kind, q=None):
    return ONCE.index(kind) if q is None else len(ONCE) + q * len(EACH) + EACH.index(kind)


def split(value):
    hi = value.astype(jnp.bfloat16)
    return hi, (value - hi.astype(jnp.float32)).astype(jnp.bfloat16)


def kernel(
    in_ref, out_ref,
    raw, rhi, rlo, cols, chi, clo, relay_a, relay_b, tile, zhalf, zfull, fin_out, fin,
    msum, m1, m2, mean, send_sem, recv_sem,
):
    samp, par = lax.axis_index("samp"), lax.axis_index("par")
    core, x, yhi = lax.rem(samp, 2), lax.rem(lax.div(samp, 2), NX), lax.div(samp, 2 * NX)
    z, ylo = lax.div(par, 2), lax.rem(par, 2)
    y = 2 * yhi + ylo
    other = 1 - core
    yb = y + 1 - 2 * ylo
    yo = lax.rem(y + 3 + 2 * ylo, NY)
    yd = lax.rem(y + 2, NY)
    xp, xm, xd = (lax.rem(x + d, NX) for d in (1, 3, 2))
    zp, zm = lax.rem(z + 1, NZ), lax.rem(z + NZ - 1, NZ)

    def dev(x=x, y=y, z=z, core=core):
        return (lax.div(y, 2) * (2 * NX) + x * 2 + core, z * 2 + lax.rem(y, 2))

    sib = dev(core=other)
    to_yb, to_yo, to_yd = dev(y=yb), dev(y=yo), dev(y=yd)
    to_xp, to_xm, to_xd = dev(x=xp), dev(x=xm), dev(x=xd)
    to_zp, to_zm = dev(z=zp), dev(z=zm)

    sent = []

    def copy(kind, q, src, dst, to):
        i = slot(kind, q)
        return pltpu.make_async_remote_copy(
            src_ref=src, dst_ref=dst, send_sem=send_sem.at[i], recv_sem=recv_sem.at[i], device_id=to, device_id_type=MESH
        )

    def send(kind, q, src, dst, to):
        c = copy(kind, q, src, dst, to)
        c.start()
        sent.append(c)

    def arrived(kind, q, ref):
        copy(kind, q, ref, ref, sib).wait_recv()

    barrier = pltpu.get_barrier_semaphore()
    peers = (sib, to_yb, to_yo, to_yd, to_xp, to_xm, to_xd, to_zp, to_zm)
    for peer in peers:
        pl.semaphore_signal(barrier, inc=1, device_id=peer, device_id_type=MESH)

    def at(start, size):
        return pl.ds(pl.multiple_of(start, 8), size)

    msum[...] = jnp.zeros_like(msum)

    @pl.loop(0, 8)
    def _(i):
        acc = msum[0]
        rows = at(core * UNIT + i * 64, 64)
        for s in range(2):
            part = in_ref[s, at(i * 64, 64), :]
            raw[ylo, rows, s * PART:(s + 1) * PART] = part
            msum[0, :, s * PART:(s + 1) * PART] = acc[:, s * PART:(s + 1) * PART] + jnp.sum(part.reshape(8, 8, PART), axis=0)

    pl.semaphore_wait(barrier, len(peers))

    def exchange(kind, half):
        rows = at(core * UNIT + half * HALF, HALF)
        send(kind, None, raw.at[ylo, rows], raw.at[ylo, rows], sib)

    exchange("sib0", other)
    exchange("sib1", core)
    arrived("sib0", None, raw.at[ylo, at(other * UNIT + core * HALF, HALF)])

    def chunk_rows(colour, q):
        return at(colour * UNIT + core * HALF + q * CH, CH)

    def piece(x, rel, q):
        return cols.at[q, x, at(rel * CH, CH)]

    def send_y(q):
        away = raw.at[ylo, chunk_rows(1 - ylo, q)]
        send("oa", q, away, piece(x, 2 * ylo, q), to_yb)
        send("ob", q, away, piece(x, 2 - 2 * ylo, q), to_yo)
        rows = raw.at[ylo, chunk_rows(ylo, q)]
        send("j0", q, rows, rows, to_yb)

    send_y(0)
    arrived("sib1", None, raw.at[ylo, at(other * UNIT + other * HALF, HALF)])

    @pl.loop(0, 8)
    def _(i):
        part = raw[ylo, at(other * UNIT + i * 64, 64), :]
        msum[0] = msum[0] + jnp.sum(part.reshape(8, 8, KU), axis=0)

    send("m1a", None, msum.at[0], m1.at[0], to_yb)
    send("m1b", None, msum.at[0], m1.at[1], to_yo)
    send("m1c", None, msum.at[0], m1.at[2], to_yd)
    for q in range(1, N):
        send_y(q)
    for i, kind in enumerate(("m1a", "m1b", "m1c")):
        arrived(kind, None, m1.at[i])
    m2[0, ylo] = msum[0] + m1[2]
    m2[0, 1 - ylo] = m1[0] + m1[1]
    send("m2a", None, m2.at[0], m2.at[1], to_xp)
    send("m2b", None, m2.at[0], m2.at[2], to_xm)
    send("m2c", None, m2.at[0], m2.at[3], to_xd)

    def send_x(q):
        arrived("oa", q, piece(x, 2 - 2 * ylo, q))
        arrived("ob", q, piece(x, 2 * ylo, q))
        cols[q, x, CH:2 * CH, :] = raw[ylo, chunk_rows(ylo, q), :]
        own = cols.at[q, x, 0:3 * CH]
        send("xr", q, own, own, to_xp)
        send("xl", q, own, own, to_xm)
        raw[1 - ylo, chunk_rows(ylo, q), :] = cols[q, x, at((2 - 2 * ylo) * CH, CH), :]
        passed = raw.at[1 - ylo, chunk_rows(1 - ylo, q)]
        arrived("j0", q, passed)
        send("g0", q, passed, piece(x, 3, q), to_yo)

    cut = 3 * CH // 2

    def forward_x(q):
        arrived("xr", q, cols.at[q, xm, 0:3 * CH])
        low = cols.at[q, xm, 0:cut]
        send("fr", q, low, low, to_xp)
        arrived("xl", q, cols.at[q, xp, 0:3 * CH])
        high = cols.at[q, xp, cut:3 * CH]
        send("fl", q, high, high, to_xm)
        send("j1", q, piece(xm, 1, q), relay_b.at[q, 0], to_yo)
        send("j2", q, piece(xp, 1, q), relay_b.at[q, 1], to_yo)

    def end_x(q):
        arrived("fr", q, cols.at[q, xd, 0:cut])
        arrived("fl", q, cols.at[q, xd, cut:3 * CH])
        send("j3", q, piece(xd, 1, q), relay_a.at[q], to_yb)

    def relays(q):
        arrived("j1", q, relay_b.at[q, 0])
        send("g1", q, relay_b.at[q, 0], piece(xm, 3, q), to_yb)
        arrived("j2", q, relay_b.at[q, 1])
        send("g2", q, relay_b.at[q, 1], piece(xp, 3, q), to_yb)
        arrived("j3", q, relay_a.at[q])
        send("g3", q, relay_a.at[q], piece(xd, 3, q), to_yo)

    def rows_ready():
        for c in range(2):
            rows = at(c * UNIT + core * HALF, HALF)
            send(f"row{c}", None, raw.at[1 - ylo, rows], raw.at[1 - ylo, rows], sib)
        for i, kind in enumerate(("m2a", "m2b", "m2c")):
            arrived(kind, None, m2.at[i + 1])
        total = (m2[0] + m2[1]) + (m2[2] + m2[3])
        mean[...] = jnp.sum(total, axis=1, keepdims=True) / SAMPLES
        for c in range(2):
            arrived(f"row{c}", None, raw.at[1 - ylo, at(c * UNIT + other * HALF, HALF)])

        @pl.loop(0, 16)
        def _(i):
            rows = at(i * 64, 64)
            for p in range(2):
                hi, lo = split(raw[p, rows, :] - mean[p])
                rhi[rows, p * KU:(p + 1) * KU] = hi
                rlo[rows, p * KU:(p + 1) * KU] = lo

    def product(q):
        arrived("g0", q, piece(x, 3, q))
        arrived("g1", q, piece(xm, 3, q))
        arrived("g2", q, piece(xp, 3, q))
        arrived("g3", q, piece(xd, 3, q))

        @pl.loop(0, 8)
        def _(s):
            to = pl.ds(pl.multiple_of(s * CH, CH), CH)
            for p in range(2):
                rel = lax.rem(2 * lax.div(s, NX) + p - y + 5, NY)
                value = cols[q, lax.rem(s, NX), at(rel * CH, CH), :]
                hi, lo = split(value - mean[p])
                chi[to, p * KU:(p + 1) * KU] = hi
                clo[to, p * KU:(p + 1) * KU] = lo

        dims = (((1,), (1,)), ((), ()))
        dot = functools.partial(lax.dot_general, dimension_numbers=dims, preferred_element_type=jnp.float32)

        @pl.loop(0, 4)
        def _(r):
            lanes = pl.ds(pl.multiple_of(r * 256, 256), 256)
            ch, rh = chi[...], rhi[lanes, :]
            tile[q, :, lanes] = dot(ch, rh) + dot(ch, rlo[lanes, :]) + dot(clo[...], rh)

    def block(q, step):
        return at(lax.rem(z + step + NZ, NZ) * CH, CH)

    def reduce0(q):
        rows = block(q, 4)
        send("z0p", q, tile.at[q, rows, UNIT:2 * UNIT], zhalf.at[q, 0], to_zp)
        send("z0m", q, tile.at[q, rows, 0:UNIT], zhalf.at[q, 1], to_zm)

    def reduce1(q):
        for d, kind, nxt, to, lanes, step in (
            (0, "z0p", "z1p", to_zp, slice(UNIT, 2 * UNIT), 3), (1, "z0m", "z1m", to_zm, slice(0, UNIT), -3),
        ):
            arrived(kind, q, zhalf.at[q, d])
            rows = block(q, step)
            tile[q, rows, lanes] = tile[q, rows, lanes] + zhalf[q, d]
            send(nxt, q, tile.at[q, rows], zfull.at[q, d, 0], to)

    def reduce_mid(q, i):
        for d, tag, to, step in ((0, "p", to_zp, 3 - i), (1, "m", to_zm, i - 3)):
            arrived(f"z{i}{tag}", q, zfull.at[q, d, i - 1])
            rows = block(q, step)
            tile[q, rows, :] = tile[q, rows, :] + zfull[q, d, i - 1]
            send(f"z{i + 1}{tag}", q, tile.at[q, rows], zfull.at[q, d, i], to)

    def reduce_end(q):
        arrived("z3p", q, zfull.at[q, 0, 2])
        arrived("z3m", q, zfull.at[q, 1, 2])
        total = (tile[q, block(q, 0), :] + (zfull[q, 0, 2] + zfull[q, 1, 2])) * SCALE
        low, high = total[:, :UNIT], total[:, UNIT:]
        first = core == 0
        fin[at(core * HALF + q * CH, CH), :] = jnp.where(first, low, high)
        fin_out[q] = jnp.where(first, high, low)
        send("fin", q, fin_out.at[q], fin.at[at(core * HALF + q * CH, CH)], sib)

    send_x(0)
    send_x(1)
    forward_x(0)
    send_x(2)
    end_x(0)
    send_x(3)
    rows_ready()
    relays(0)
    forward_x(1)
    product(0)
    reduce0(0)
    end_x(1)
    forward_x(2)
    relays(1)
    reduce1(0)
    product(1)
    reduce0(1)
    reduce_mid(0, 1)
    end_x(2)
    forward_x(3)
    relays(2)
    reduce1(1)
    reduce_mid(0, 2)
    product(2)
    reduce0(2)
    reduce_mid(1, 1)
    end_x(3)
    reduce_end(0)
    relays(3)
    reduce1(2)
    reduce_mid(1, 2)
    product(3)
    reduce0(3)
    reduce_mid(2, 1)
    reduce_end(1)
    reduce1(3)
    reduce_mid(2, 2)
    reduce_mid(3, 1)
    reduce_end(2)
    reduce_mid(3, 2)
    reduce_end(3)
    for q in range(N):
        arrived("fin", q, fin.at[at(other * HALF + q * CH, CH)])
    out_ref[...] = fin[...].T
    for c in sent:
        c.wait_send()


def shards(log_derivs):
    f32, bf16, VMEM = jnp.float32, jnp.bfloat16, pltpu.VMEM
    rows, depth, width = 2 * UNIT, 2 * KU, 8 * CH
    scratch = [
        VMEM((2, rows, KU), f32), VMEM((rows, depth), bf16), VMEM((rows, depth), bf16),
        VMEM((N, NX, 4 * CH, KU), f32), VMEM((width, depth), bf16), VMEM((width, depth), bf16),
        VMEM((N, CH, KU), f32), VMEM((N, 2, CH, KU), f32),
        VMEM((N, width, rows), f32), VMEM((N, 2, CH, UNIT), f32), VMEM((N, 2, 3, CH, rows), f32),
        VMEM((N, CH, UNIT), f32), VMEM((UNIT, UNIT), f32),
        VMEM((1, 8, KU), f32), VMEM((3, 8, KU), f32), VMEM((4, 2, 8, KU), f32), VMEM((2, 1, KU), f32),
        pltpu.SemaphoreType.DMA((SEMS,)), pltpu.SemaphoreType.DMA((SEMS,)),
    ]
    return pl.pallas_call(
        kernel,
        out_shape=jax.ShapeDtypeStruct((UNIT, UNIT), f32),
        in_specs=[pl.BlockSpec(memory_space=VMEM)],
        out_specs=pl.BlockSpec(memory_space=VMEM),
        scratch_shapes=scratch,
        compiler_params=pltpu.CompilerParams(collective_id=0, has_side_effects=True, vmem_limit_bytes=60 * 2**20),
        cost_estimate=pl.CostEstimate(flops=20 * 10**9, bytes_accessed=4 * 2**20, transcendentals=0),
    )(log_derivs)


def solution(mesh):
    in_specs = (P(None, "samp", "par"),)
    out_specs = P("samp", "par")
    return jax.shard_map(shards, mesh=mesh, in_specs=in_specs, out_specs=out_specs, check_vma=False)
```

```python
import functools

import jax
import jax.numpy as jnp
from jax import lax
from jax.experimental import pallas as pl
from jax.experimental.pallas import tpu as pltpu
from jax.sharding import PartitionSpec as P

MESH = pl.DeviceIdType.MESH
NX, NY, NZ = 4, 4, 8
UNIT = 512
HALF = UNIT // 2
PART = 384
KEEP = 3
KU = 2 * PART
SIZES = (32, 32, 32, 32, 32, 32, 32, 32)
N = len(SIZES)
START = tuple(sum(SIZES[:q]) for q in range(N))
SAMPLES = 8192
SCALE = 1.0 / 12288.0
ACROSS = (False, False, True, True, True, True, True, True)
GROUP = 64
GROUPS = HALF // GROUP
PARTS = (
    (0, 0, 1), (0, 1, 1), (1, 0, 2), (0, 2, 1), (1, 2, 1), (0, 3, 1), (1, 3, 1), (2, 0, 4), (3, 0, 4), (4, 0, 4),
    (5, 0, 4), (6, 0, 4), (7, 0, 2), (7, 2, 2),
)

ONCE = ["sib0", "sib1", "m1a", "m1b", "m1c", "m2a", "m2b", "m2c"] + [f"row{i}" for i in range(2 * GROUPS)]
EACH = [
    "oa", "ob", "j0", "g0", "xr0", "xl0", "fr0", "fl0", "xr1", "xl1", "fr1", "fl1", "xr2", "xl2", "fr2", "fl2",
]
REDUCE = ["z0p", "z0m", "z1p", "z1m", "z2p", "z2m", "z3p", "z3m", "fin"]
SEMS = len(ONCE) + N * len(EACH) + len(PARTS) * len(REDUCE)

ORDER = (
    (3, 0), (4, 0), (5, 0), (5, 2), (4, 1), (0, 0), (3, 1), (3, 2), (3, 3), (6, 0), (8, 0), (7, 0), (10, 2), (4, 3),
    (3, 4), (4, 5), (3, 5), (3, 6), (3, 7), (10, 0), (1, 0), (6, 1), (9, 0), (5, 1), (11, 0), (7, 1), (2, 0), (12,
    0), (7, 2), (4, 7), (13, 0), (9, 1), (8, 1), (6, 2), (6, 3), (4, 6), (12, 2), (4, 2), (4, 4), (10, 1), (14, 2),
    (15, 2), (5, 3), (7, 3), (2, 1), (13, 1), (6, 4), (16, 0), (17, 0), (17, 1), (18, 0), (6, 5), (18, 1), (11, 1),
    (7, 4), (7, 5), (2, 2), (19, 0), (5, 4), (8, 2), (19, 1), (12, 1), (16, 1), (17, 2), (18, 2), (10, 3), (14, 3),
    (17, 3), (18, 3), (17, 4), (18, 4), (6, 7), (20, 0), (19, 2), (6, 6), (8, 3), (7, 7), (7, 6), (2, 3), (17, 5),
    (18, 5), (20, 2), (12, 3), (15, 3), (11, 2), (19, 4), (19, 3), (8, 4), (17, 6), (18, 6), (19, 5), (20, 1), (10,
    4), (21, 2), (9, 3), (14, 4), (21, 0), (20, 4), (9, 2), (11, 3), (20, 3), (19, 6), (16, 2), (17, 7), (18, 7),
    (20, 5), (5, 5), (8, 5), (21, 1), (21, 4), (16, 3), (20, 6), (19, 7), (17, 8), (18, 8), (12, 4), (15, 4), (11,
    4), (5, 6), (21, 5), (21, 3), (21, 6), (10, 5), (20, 7), (14, 5), (19, 8), (8, 6), (9, 4), (16, 4), (17, 9),
    (18, 9), (10, 6), (12, 5), (15, 5), (21, 7), (22, 4), (9, 6), (11, 5), (5, 7), (22, 5), (19, 9), (12, 6), (15,
    6), (20, 8), (22, 1), (22, 0), (8, 7), (9, 5), (16, 5), (14, 6), (10, 7), (14, 7), (11, 6), (20, 9), (17, 10),
    (18, 10), (21, 8), (12, 7), (15, 7), (11, 7), (22, 6), (21, 9), (16, 6), (17, 11), (18, 11), (19, 10), (9, 7),
    (16, 7), (17, 12), (18, 12), (19, 11), (20, 10), (19, 12), (22, 2), (17, 13), (18, 13), (22, 3), (20, 11), (20,
    12), (19, 13), (22, 8), (22, 9), (21, 10), (20, 13), (21, 12), (21, 11), (21, 13), (22, 7), (22, 12), (22, 10),
    (22, 11), (22, 13),
)


def slot(kind, q=None):
    if q is None:
        return ONCE.index(kind)
    if kind in REDUCE:
        return len(ONCE) + N * len(EACH) + q * len(REDUCE) + REDUCE.index(kind)
    return len(ONCE) + q * len(EACH) + EACH.index(kind)


def split(value):
    hi = value.astype(jnp.bfloat16)
    return hi, (value - hi.astype(jnp.float32)).astype(jnp.bfloat16)


def kernel(
    in_ref, out_ref,
    raw, rhi, rlo, cols, chi, clo, tile, zhalf, zfull, fin_out, fin,
    msum, m1, m2, mean, send_sem, recv_sem,
):
    samp, par = lax.axis_index("samp"), lax.axis_index("par")
    core, x, yhi = lax.rem(samp, 2), lax.rem(lax.div(samp, 2), NX), lax.div(samp, 2 * NX)
    z, ylo = lax.div(par, 2), lax.rem(par, 2)
    y = 2 * yhi + ylo
    other = 1 - core
    yb = y + 1 - 2 * ylo
    yo = lax.rem(y + 3 + 2 * ylo, NY)
    yd = lax.rem(y + 2, NY)
    xp, xm, xd = (lax.rem(x + d, NX) for d in (1, 3, 2))
    zp, zm = lax.rem(z + 1, NZ), lax.rem(z + NZ - 1, NZ)

    def dev(x=x, y=y, z=z, core=core):
        return (lax.div(y, 2) * (2 * NX) + x * 2 + core, z * 2 + lax.rem(y, 2))

    sib = dev(core=other)
    to_yb, to_yo, to_yd = dev(y=yb), dev(y=yo), dev(y=yd)
    to_xp, to_xm, to_xd = dev(x=xp), dev(x=xm), dev(x=xd)
    to_zp, to_zm = dev(z=zp), dev(z=zm)

    sent = []

    def copy(kind, q, src, dst, to):
        i = slot(kind, q)
        return pltpu.make_async_remote_copy(
            src_ref=src, dst_ref=dst, send_sem=send_sem.at[i], recv_sem=recv_sem.at[i], device_id=to, device_id_type=MESH
        )

    def send(kind, q, src, dst, to):
        c = copy(kind, q, src, dst, to)
        c.start()
        sent.append(c)

    def arrived(kind, q, ref):
        copy(kind, q, ref, ref, sib).wait_recv()

    barrier = pltpu.get_barrier_semaphore()
    peers = (sib, to_yb, to_yo, to_yd, to_xp, to_xm, to_xd, to_zp, to_zm)
    for peer in peers:
        pl.semaphore_signal(barrier, inc=1, device_id=peer, device_id_type=MESH)

    def at(start, size):
        return pl.ds(pl.multiple_of(start, 8), size)

    def chunk_rows(colour, q):
        return at(colour * UNIT + core * HALF + START[q], SIZES[q])

    def piece(x, rel, q, size=1):
        return cols.at[x, at(4 * START[q] + rel * SIZES[q], size * SIZES[q])]

    def send_yo(q):
        send("ob", q, raw.at[ylo, chunk_rows(1 - ylo, q)], piece(x, 1 - ylo, q), to_yo)

    def send_yb(q):
        send("oa", q, raw.at[ylo, chunk_rows(1 - ylo, q)], piece(x, ylo, q), to_yb)
        rows = raw.at[ylo, chunk_rows(ylo, q)]
        send("j0", q, rows, rows, to_yb)

    def send_own(q):
        own = piece(x, 2, q)
        own[...] = raw[ylo, chunk_rows(ylo, q), :]
        send("xr0", q, own, own, to_xp)
        send("xl0", q, own, own, to_xm)

    def recv_next(q):
        arrived("oa", q, piece(x, 1 - ylo, q))
        raw[1 - ylo, chunk_rows(ylo, q), :] = piece(x, 1 - ylo, q)[...]

    def send_next(q):
        arrived("ob", q, piece(x, ylo, q))
        both = piece(x, 0, q, 2)
        send("xr1", q, both, both, to_xp)
        send("xl1", q, both, both, to_xm)

    def pass_far(q):
        passed = raw.at[1 - ylo, chunk_rows(1 - ylo, q)]
        arrived("j0", q, passed)
        send("g0", q, passed, piece(x, 3, q), to_yo)

    def send_far(q):
        arrived("g0", q, piece(x, 3, q))
        if not ACROSS[q]:
            far = piece(x, 3, q)
            send("xr2", q, far, far, to_xp)
            send("xl2", q, far, far, to_xm)

    def halves(rel, x, q):
        h = SIZES[q] // 2
        first = 4 * START[q] + rel * SIZES[q]
        return cols.at[x, at(first, h)], cols.at[x, at(first + h, h)]

    def forward_one(i, rel, q):
        arrived(f"xr{i}", q, piece(xm, rel, q))
        low = halves(rel, xm, q)[0]
        send(f"fr{i}", q, low, low, to_xp)
        arrived(f"xl{i}", q, piece(xp, rel, q))
        high = halves(rel, xp, q)[1]
        send(f"fl{i}", q, high, high, to_xm)

    def end_one(i, rel, q):
        low, high = halves(rel, xd, q)
        arrived(f"fr{i}", q, low)
        arrived(f"fl{i}", q, high)

    def forward_own(q):
        forward_one(0, 2, q)

    def across1(q):
        send("xr2", q, piece(xm, 2, q), piece(xm, 3, q), to_yd)
        send("xl2", q, piece(xp, 2, q), piece(xp, 3, q), to_yd)

    def across2(q):
        send("fr2", q, piece(xd, 2, q), piece(xd, 3, q), to_yd)

    def end_own(q):
        end_one(0, 2, q)

    def forward_next(q):
        arrived("xr1", q, piece(xm, 0, q, 2))
        low = piece(xm, 0, q)
        send("fr1", q, low, low, to_xp)
        arrived("xl1", q, piece(xp, 0, q, 2))
        high = piece(xp, 1, q)
        send("fl1", q, high, high, to_xm)

    def forward_far(q):
        forward_one(2, 3, q)

    def columns_ready(q):
        arrived("fr1", q, piece(xd, 0, q))
        arrived("fl1", q, piece(xd, 1, q))
        if ACROSS[q]:
            arrived("xr2", q, piece(xm, 3, q))
            arrived("xl2", q, piece(xp, 3, q))
            arrived("fr2", q, piece(xd, 3, q))
        else:
            end_one(2, 3, q)

    def send_rows(j):
        for c in range(2):
            rows = at(c * UNIT + core * HALF + j * GROUP, GROUP)
            send(f"row{2 * j + c}", None, raw.at[1 - ylo, rows], raw.at[1 - ylo, rows], sib)

    def rows_ready(j):
        send_rows(j)
        if j == 0:
            for i, kind in enumerate(("m2a", "m2b", "m2c")):
                arrived(kind, None, m2.at[i + 1])
            total = (m2[0] + m2[1]) + (m2[2] + m2[3])
            mean[...] = jnp.sum(total, axis=1, keepdims=True) / SAMPLES
        for c in range(2):
            arrived(f"row{2 * j + c}", None, raw.at[1 - ylo, at(c * UNIT + other * HALF + j * GROUP, GROUP)])

        @pl.loop(0, GROUP // 16)
        def _(i):
            n = GROUP // 64
            src = at(lax.div(i, n) * HALF + j * GROUP + lax.rem(i, n) * 64, 64)
            dst = at(j * 4 * GROUP + i * 64, 64)
            for p in range(2):
                hi, lo = split(raw[p, src, :] - mean[p])
                rhi[dst, p * KU:(p + 1) * KU] = hi
                rlo[dst, p * KU:(p + 1) * KU] = lo

    def columns(q):
        columns_ready(q)
        keep, size = q % KEEP, SIZES[q]

        @pl.loop(0, 8)
        def _(s):
            to = pl.ds(pl.multiple_of(s * size, 16), size)
            for p in range(2):
                off = lax.rem(2 * lax.div(s, NX) + p - y + NY, NY)
                rel = jnp.where(off == 0, 2, jnp.where(off == 1, 1, jnp.where(off == 2, 3, 0)))
                hi, lo = split(piece(lax.rem(s, NX), rel, q)[...] - mean[p])
                chi[keep, to, p * KU:(p + 1) * KU] = hi
                clo[keep, to, p * KU:(p + 1) * KU] = lo

    dims = (((1,), (1,)), ((), ()))
    dot = functools.partial(lax.dot_general, dimension_numbers=dims, preferred_element_type=jnp.float32)

    def product(u):
        q, j0, count = PARTS[u]
        keep, width = q % KEEP, 8 * SIZES[q]

        @pl.loop(0, count * GROUP // 64)
        def _(r):
            rows = pl.ds(pl.multiple_of(j0 * 4 * GROUP + r * HALF, HALF), HALF)
            n = GROUP // 64
            lanes = pl.ds(pl.multiple_of(lax.rem(r, n) * HALF, HALF), HALF)
            ch, rh = chi[keep, :width], rhi[rows, :]
            tile[j0 + lax.div(r, n), 8 * START[q]:8 * START[q] + width, lanes] = (
                dot(ch, rh) + dot(ch, rlo[rows, :]) + dot(clo[keep, :width], rh)
            )

    def block(u, step, lanes=slice(None)):
        q, j0, count = PARTS[u]
        rows = at(8 * START[q] + lax.rem(z + step + NZ, NZ) * SIZES[q], SIZES[q])
        return tile.at[j0:j0 + count, rows, lanes]

    def full(u, d, i):
        q, j0, count = PARTS[u]
        return zfull.at[d, i, j0:j0 + count, START[q]:START[q] + SIZES[q]]

    def half(u, d):
        q, j0, count = PARTS[u]
        return zhalf.at[d, j0:j0 + count, START[q]:START[q] + SIZES[q]]

    low, high = slice(0, 2 * GROUP), slice(2 * GROUP, 4 * GROUP)

    def reduce0(u):
        send("z0p", u, block(u, 4, high), half(u, 0), to_zp)
        send("z0m", u, block(u, 4, low), half(u, 1), to_zm)

    def reduce1(u):
        for d, tag, to, lanes, step in ((0, "p", to_zp, high, 3), (1, "m", to_zm, low, -3)):
            arrived(f"z0{tag}", u, half(u, d))
            part = block(u, step, lanes)
            part[...] = part[...] + half(u, d)[...]
            send(f"z1{tag}", u, block(u, step), full(u, d, 0), to)

    def reduce_mid(u, i):
        for d, tag, to, step in ((0, "p", to_zp, 3 - i), (1, "m", to_zm, i - 3)):
            arrived(f"z{i}{tag}", u, full(u, d, i - 1))
            part = block(u, step)
            part[...] = part[...] + full(u, d, i - 1)[...]
            send(f"z{i + 1}{tag}", u, part, full(u, d, i), to)

    def final(u, c):
        q, j0, count = PARTS[u]
        return fin.at[j0:j0 + count, at(c * HALF + START[q], SIZES[q])]

    def reduce_end(u):
        q, j0, count = PARTS[u]
        arrived("z3p", u, full(u, 0, 2))
        arrived("z3m", u, full(u, 1, 2))
        total = (block(u, 0)[...] + (full(u, 0, 2)[...] + full(u, 1, 2)[...])) * SCALE
        first = core == 0
        final(u, core)[...] = jnp.where(first, total[..., low], total[..., high])
        away = fin_out.at[j0:j0 + count, START[q]:START[q] + SIZES[q]]
        away[...] = jnp.where(first, total[..., high], total[..., low])
        send("fin", u, away, final(u, core), sib)

    def exchange(kind, half):
        rows = at(core * UNIT + half * HALF, HALF)
        send(kind, None, raw.at[ylo, rows], raw.at[ylo, rows], sib)

    def means1():
        arrived("sib1", None, raw.at[ylo, at(other * UNIT + other * HALF, HALF)])
        msum[...] = jnp.zeros_like(msum)

        @pl.loop(0, 16)
        def _(i):
            part = raw[ylo, at(i * 64, 64), :]
            msum[0] = msum[0] + jnp.sum(part.reshape(8, 8, KU), axis=0)

        send("m1a", None, msum.at[0], m1.at[0], to_yb)
        send("m1b", None, msum.at[0], m1.at[1], to_yo)
        send("m1c", None, msum.at[0], m1.at[2], to_yd)

    def means2():
        for i, kind in enumerate(("m1a", "m1b", "m1c")):
            arrived(kind, None, m1.at[i])
        m2[0, ylo] = msum[0] + m1[2]
        m2[0, 1 - ylo] = m1[0] + m1[1]
        send("m2a", None, m2.at[0], m2.at[1], to_xp)
        send("m2b", None, m2.at[0], m2.at[2], to_xm)
        send("m2c", None, m2.at[0], m2.at[3], to_xd)

    @pl.loop(0, 8)
    def _(i):
        for s in range(2):
            raw[ylo, at(core * UNIT + i * 64, 64), s * PART:(s + 1) * PART] = in_ref[s, at(i * 64, 64), :]

    pl.semaphore_wait(barrier, len(peers))
    exchange("sib0", other)
    exchange("sib1", core)
    arrived("sib0", None, raw.at[ylo, at(other * UNIT + core * HALF, HALF)])

    steps = (
        lambda _: means1(), lambda _: means2(), rows_ready,
        send_yb, send_yo, send_own, recv_next, pass_far, send_next, send_far, forward_own, forward_next, end_own,
        forward_far, across1, across2, columns, product, reduce0, reduce1,
        lambda u: reduce_mid(u, 1), lambda u: reduce_mid(u, 2), reduce_end,
    )
    for step, index in ORDER:
        steps[step](index)
    for u in range(len(PARTS)):
        arrived("fin", u, final(u, other))
    for j in range(GROUPS):
        turned = fin[j].T
        for h in range(2):
            out_ref[h * HALF + j * GROUP:h * HALF + (j + 1) * GROUP, :] = turned[h * GROUP:(h + 1) * GROUP]
    for c in sent:
        c.wait_send()


def shards(log_derivs):
    f32, bf16, VMEM = jnp.float32, jnp.bfloat16, pltpu.VMEM
    rows, depth, width = 2 * UNIT, 2 * KU, 8 * max(SIZES)
    scratch = [
        VMEM((2, rows, KU), f32), VMEM((rows, depth), bf16), VMEM((rows, depth), bf16),
        VMEM((NX, 4 * HALF, KU), f32), VMEM((KEEP, width, depth), bf16), VMEM((KEEP, width, depth), bf16),
        VMEM((GROUPS, 8 * HALF, 4 * GROUP), f32),
        VMEM((2, GROUPS, HALF, 2 * GROUP), f32), VMEM((2, 3, GROUPS, HALF, 4 * GROUP), f32),
        VMEM((GROUPS, HALF, 2 * GROUP), f32), VMEM((GROUPS, UNIT, 2 * GROUP), f32),
        VMEM((1, 8, KU), f32), VMEM((3, 8, KU), f32), VMEM((4, 2, 8, KU), f32), VMEM((2, 1, KU), f32),
        pltpu.SemaphoreType.DMA((SEMS,)), pltpu.SemaphoreType.DMA((SEMS,)),
    ]
    return pl.pallas_call(
        kernel,
        out_shape=jax.ShapeDtypeStruct((UNIT, UNIT), f32),
        in_specs=[pl.BlockSpec(memory_space=VMEM)],
        out_specs=pl.BlockSpec(memory_space=VMEM),
        scratch_shapes=scratch,
        compiler_params=pltpu.CompilerParams(collective_id=0, has_side_effects=True, vmem_limit_bytes=60 * 2**20),
        cost_estimate=pl.CostEstimate(flops=20 * 10**9, bytes_accessed=4 * 2**20, transcendentals=0),
    )(log_derivs)


def solution(mesh):
    in_specs = (P(None, "samp", "par"),)
    out_specs = P("samp", "par")
    return jax.shard_map(shards, mesh=mesh, in_specs=in_specs, out_specs=out_specs, check_vma=False)
```

```python
import functools

import jax
import jax.numpy as jnp
from jax import lax
from jax.experimental import pallas as pl
from jax.experimental.pallas import tpu as pltpu
from jax.sharding import PartitionSpec as P

MESH = pl.DeviceIdType.MESH
NX, NY, NZ = 4, 4, 8
UNIT = 512
HALF = UNIT // 2
PART = 384
KEEP = 3
KU = 2 * PART
SIZES = (32, 32, 32, 32, 32, 32, 32, 32)
N = len(SIZES)
START = tuple(sum(SIZES[:q]) for q in range(N))
SAMPLES = 8192
SCALE = 1.0 / 12288.0
ACROSS = (False, False, True, True, True, True, True, True)
GROUP = 64
GROUPS = HALF // GROUP
EARLY = (0,)
PARTS = (
    (0, 0, 1), (0, 1, 1), (1, 0, 2), (0, 2, 1), (1, 2, 1), (0, 3, 1), (1, 3, 1), (2, 0, 4), (3, 0, 4), (4, 0, 4),
    (5, 0, 4), (6, 0, 4), (7, 0, 2), (7, 2, 2),
)

LAG = 70

ONCE = ["sib0", "sib1", "m1a", "m1b", "m1c", "m2a", "m2b", "m2c"] + [f"row{i}" for i in range(2 * GROUPS)]
EACH = [
    "oa", "ob", "j0", "g0", "xr0", "xl0", "fr0", "fl0", "xr1", "xl1", "fr1", "fl1", "xr2", "xl2", "fr2", "fl2",
]
REDUCE = ["z0p", "z0m", "z1p", "z1m", "z2p", "z2m", "z3p", "z3m", "fin"]
SEMS = len(ONCE) + N * len(EACH) + len(PARTS) * len(REDUCE)

ORDER = (
    (4, 0), (5, 0), (6, 0), (6, 2), (5, 1), (0, 0), (4, 1), (4, 2), (4, 3), (7, 0), (9, 0), (8, 0), (11, 2), (5, 3),
    (4, 4), (5, 5), (4, 5), (4, 6), (4, 7), (11, 0), (1, 0), (7, 1), (10, 0), (6, 1), (12, 0), (8, 1), (2, 0), (3,
    0), (13, 0), (8, 2), (5, 7), (14, 0), (10, 1), (9, 1), (7, 2), (7, 3), (5, 6), (13, 2), (5, 2), (5, 4), (11, 1),
    (15, 2), (16, 2), (6, 3), (8, 3), (2, 1), (3, 1), (14, 1), (7, 4), (17, 0), (18, 0), (18, 1), (19, 0), (7, 5),
    (19, 1), (12, 1), (8, 4), (8, 5), (2, 2), (3, 2), (20, 0), (6, 4), (9, 2), (20, 1), (13, 1), (17, 1), (18, 2),
    (19, 2), (11, 3), (15, 3), (18, 3), (19, 3), (18, 4), (19, 4), (7, 7), (21, 0), (20, 2), (7, 6), (9, 3), (8, 7),
    (8, 6), (2, 3), (3, 3), (18, 5), (19, 5), (21, 2), (13, 3), (16, 3), (12, 2), (20, 4), (20, 3), (9, 4), (18, 6),
    (19, 6), (20, 5), (21, 1), (11, 4), (22, 2), (10, 3), (15, 4), (22, 0), (21, 4), (10, 2), (12, 3), (21, 3), (20,
    6), (17, 2), (18, 7), (19, 7), (21, 5), (6, 5), (9, 5), (22, 1), (22, 4), (17, 3), (21, 6), (20, 7), (18, 8),
    (19, 8), (13, 4), (16, 4), (12, 4), (6, 6), (22, 5), (22, 3), (22, 6), (11, 5), (21, 7), (15, 5), (20, 8), (9,
    6), (10, 4), (17, 4), (18, 9), (19, 9), (11, 6), (13, 5), (16, 5), (22, 7), (23, 4), (10, 6), (12, 5), (6, 7),
    (23, 5), (20, 9), (13, 6), (16, 6), (21, 8), (23, 1), (23, 0), (9, 7), (10, 5), (17, 5), (15, 6), (11, 7), (15,
    7), (12, 6), (21, 9), (18, 10), (19, 10), (22, 8), (13, 7), (16, 7), (12, 7), (23, 6), (22, 9), (17, 6), (18,
    11), (19, 11), (20, 10), (10, 7), (17, 7), (18, 12), (19, 12), (20, 11), (21, 10), (20, 12), (23, 2), (18, 13),
    (19, 13), (23, 3), (21, 11), (21, 12), (20, 13), (23, 8), (23, 9), (22, 10), (21, 13), (22, 12), (22, 11), (22,
    13), (23, 7), (23, 12), (23, 10), (23, 11), (23, 13),
)


def slot(kind, q=None):
    if q is None:
        return ONCE.index(kind)
    if kind in REDUCE:
        return len(ONCE) + N * len(EACH) + q * len(REDUCE) + REDUCE.index(kind)
    return len(ONCE) + q * len(EACH) + EACH.index(kind)


def split(value):
    hi = value.astype(jnp.bfloat16)
    return hi, (value - hi.astype(jnp.float32)).astype(jnp.bfloat16)


def kernel(
    in_ref, out_ref,
    raw, rhi, rlo, cols, chi, clo, tile, zhalf, zfull, fin_out, fin,
    msum, m1, m2, mean, send_sem, recv_sem,
):
    samp, par = lax.axis_index("samp"), lax.axis_index("par")
    core, x, yhi = lax.rem(samp, 2), lax.rem(lax.div(samp, 2), NX), lax.div(samp, 2 * NX)
    z, ylo = lax.div(par, 2), lax.rem(par, 2)
    y = 2 * yhi + ylo
    other = 1 - core
    yb = y + 1 - 2 * ylo
    yo = lax.rem(y + 3 + 2 * ylo, NY)
    yd = lax.rem(y + 2, NY)
    xp, xm, xd = (lax.rem(x + d, NX) for d in (1, 3, 2))
    zp, zm = lax.rem(z + 1, NZ), lax.rem(z + NZ - 1, NZ)

    def dev(x=x, y=y, z=z, core=core):
        return (lax.div(y, 2) * (2 * NX) + x * 2 + core, z * 2 + lax.rem(y, 2))

    sib = dev(core=other)
    to_yb, to_yo, to_yd = dev(y=yb), dev(y=yo), dev(y=yd)
    to_xp, to_xm, to_xd = dev(x=xp), dev(x=xm), dev(x=xd)
    to_zp, to_zm = dev(z=zp), dev(z=zm)

    sent = []

    def copy(kind, q, src, dst, to):
        i = slot(kind, q)
        return pltpu.make_async_remote_copy(
            src_ref=src, dst_ref=dst, send_sem=send_sem.at[i], recv_sem=recv_sem.at[i], device_id=to, device_id_type=MESH
        )

    def send(kind, q, src, dst, to):
        go(copy(kind, q, src, dst, to))

    def go(c):
        c.start()
        sent.append(c)

    def arrived(kind, q, ref):
        copy(kind, q, ref, ref, sib).wait_recv()

    barrier = pltpu.get_barrier_semaphore()
    peers = (sib, to_yb, to_yo, to_yd, to_xp, to_xm, to_xd, to_zp, to_zm)
    for peer in peers:
        pl.semaphore_signal(barrier, inc=1, device_id=peer, device_id_type=MESH)

    def at(start, size):
        return pl.ds(pl.multiple_of(start, 8), size)

    def chunk_rows(colour, q):
        return at(colour * UNIT + core * HALF + START[q], SIZES[q])

    def piece(x, rel, q, size=1):
        return cols.at[x, at(4 * START[q] + rel * SIZES[q], size * SIZES[q])]

    def away(kind, q):
        src = raw.at[ylo, chunk_rows(1 - ylo, q)]
        if kind == "oa":
            return copy(kind, q, src, piece(x, ylo, q), to_yb)
        return copy(kind, q, src, piece(x, 1 - ylo, q), to_yo)

    def send_yo(q):
        if q not in EARLY:
            go(away("ob", q))

    def send_yb(q):
        if q not in EARLY:
            go(away("oa", q))
        rows = raw.at[ylo, chunk_rows(ylo, q)]
        send("j0", q, rows, rows, to_yb)

    def own_copies(q):
        own = piece(x, 2, q)
        return copy("xr0", q, own, own, to_xp), copy("xl0", q, own, own, to_xm)

    def place_own(q):
        own = piece(x, 2, q)
        own[...] = raw[ylo, chunk_rows(ylo, q), :]

    def send_own(q):
        if q not in EARLY:
            place_own(q)
            for c in own_copies(q):
                go(c)

    def early_own():
        for q in EARLY:
            place_own(q)
            for c in own_copies(q):
                c.start()

    def early_away():
        for q in EARLY:
            away("oa", q).start()
            away("ob", q).start()

    def recv_next(q):
        arrived("oa", q, piece(x, 1 - ylo, q))
        raw[1 - ylo, chunk_rows(ylo, q), :] = piece(x, 1 - ylo, q)[...]

    def send_next(q):
        arrived("ob", q, piece(x, ylo, q))
        both = piece(x, 0, q, 2)
        send("xr1", q, both, both, to_xp)
        send("xl1", q, both, both, to_xm)

    def pass_far(q):
        passed = raw.at[1 - ylo, chunk_rows(1 - ylo, q)]
        arrived("j0", q, passed)
        send("g0", q, passed, piece(x, 3, q), to_yo)

    def send_far(q):
        arrived("g0", q, piece(x, 3, q))
        if not ACROSS[q]:
            far = piece(x, 3, q)
            send("xr2", q, far, far, to_xp)
            send("xl2", q, far, far, to_xm)

    def halves(rel, x, q):
        h = SIZES[q] // 2
        first = 4 * START[q] + rel * SIZES[q]
        return cols.at[x, at(first, h)], cols.at[x, at(first + h, h)]

    def forward_one(i, rel, q):
        arrived(f"xr{i}", q, piece(xm, rel, q))
        low = halves(rel, xm, q)[0]
        send(f"fr{i}", q, low, low, to_xp)
        arrived(f"xl{i}", q, piece(xp, rel, q))
        high = halves(rel, xp, q)[1]
        send(f"fl{i}", q, high, high, to_xm)

    def end_one(i, rel, q):
        low, high = halves(rel, xd, q)
        arrived(f"fr{i}", q, low)
        arrived(f"fl{i}", q, high)

    def forward_own(q):
        forward_one(0, 2, q)

    def across1(q):
        send("xr2", q, piece(xm, 2, q), piece(xm, 3, q), to_yd)
        send("xl2", q, piece(xp, 2, q), piece(xp, 3, q), to_yd)

    def across2(q):
        send("fr2", q, piece(xd, 2, q), piece(xd, 3, q), to_yd)

    def end_own(q):
        end_one(0, 2, q)

    def forward_next(q):
        arrived("xr1", q, piece(xm, 0, q, 2))
        low = piece(xm, 0, q)
        send("fr1", q, low, low, to_xp)
        arrived("xl1", q, piece(xp, 0, q, 2))
        high = piece(xp, 1, q)
        send("fl1", q, high, high, to_xm)

    def forward_far(q):
        forward_one(2, 3, q)

    def columns_ready(q):
        arrived("fr1", q, piece(xd, 0, q))
        arrived("fl1", q, piece(xd, 1, q))
        if ACROSS[q]:
            arrived("xr2", q, piece(xm, 3, q))
            arrived("xl2", q, piece(xp, 3, q))
            arrived("fr2", q, piece(xd, 3, q))
        else:
            end_one(2, 3, q)

    def send_rows(j):
        for c in range(2):
            rows = at(c * UNIT + core * HALF + j * GROUP, GROUP)
            send(f"row{2 * j + c}", None, raw.at[1 - ylo, rows], raw.at[1 - ylo, rows], sib)

    def rows_ready(j):
        if j == 0:
            for i, kind in enumerate(("m2a", "m2b", "m2c")):
                arrived(kind, None, m2.at[i + 1])
            total = (m2[0] + m2[1]) + (m2[2] + m2[3])
            mean[...] = jnp.sum(total, axis=1, keepdims=True) / SAMPLES
        for c in range(2):
            arrived(f"row{2 * j + c}", None, raw.at[1 - ylo, at(c * UNIT + other * HALF + j * GROUP, GROUP)])

        @pl.loop(0, GROUP // 16)
        def _(i):
            n = GROUP // 64
            src = at(lax.div(i, n) * HALF + j * GROUP + lax.rem(i, n) * 64, 64)
            dst = at(j * 4 * GROUP + i * 64, 64)
            for p in range(2):
                hi, lo = split(raw[p, src, :] - mean[p])
                rhi[dst, p * KU:(p + 1) * KU] = hi
                rlo[dst, p * KU:(p + 1) * KU] = lo

    def columns(q):
        columns_ready(q)
        keep, size = q % KEEP, SIZES[q]

        @pl.loop(0, 8)
        def _(s):
            to = pl.ds(pl.multiple_of(s * size, 16), size)
            for p in range(2):
                off = lax.rem(2 * lax.div(s, NX) + p - y + NY, NY)
                rel = jnp.where(off == 0, 2, jnp.where(off == 1, 1, jnp.where(off == 2, 3, 0)))
                hi, lo = split(piece(lax.rem(s, NX), rel, q)[...] - mean[p])
                chi[keep, to, p * KU:(p + 1) * KU] = hi
                clo[keep, to, p * KU:(p + 1) * KU] = lo

    dims = (((1,), (1,)), ((), ()))
    dot = functools.partial(lax.dot_general, dimension_numbers=dims, preferred_element_type=jnp.float32)

    def product(u):
        q, j0, count = PARTS[u]
        keep, width = q % KEEP, 8 * SIZES[q]

        @pl.loop(0, count * GROUP // 64)
        def _(r):
            rows = pl.ds(pl.multiple_of(j0 * 4 * GROUP + r * HALF, HALF), HALF)
            n = GROUP // 64
            lanes = pl.ds(pl.multiple_of(lax.rem(r, n) * HALF, HALF), HALF)
            ch, rh = chi[keep, :width], rhi[rows, :]
            tile[j0 + lax.div(r, n), 8 * START[q]:8 * START[q] + width, lanes] = (
                dot(ch, rh) + dot(ch, rlo[rows, :]) + dot(clo[keep, :width], rh)
            )

    def block(u, step, lanes=slice(None)):
        q, j0, count = PARTS[u]
        rows = at(8 * START[q] + lax.rem(z + step + NZ, NZ) * SIZES[q], SIZES[q])
        return tile.at[j0:j0 + count, rows, lanes]

    def full(u, d, i):
        q, j0, count = PARTS[u]
        return zfull.at[d, i, j0:j0 + count, START[q]:START[q] + SIZES[q]]

    def half(u, d):
        q, j0, count = PARTS[u]
        return zhalf.at[d, j0:j0 + count, START[q]:START[q] + SIZES[q]]

    low, high = slice(0, 2 * GROUP), slice(2 * GROUP, 4 * GROUP)

    def reduce0(u):
        send("z0p", u, block(u, 4, high), half(u, 0), to_zp)
        send("z0m", u, block(u, 4, low), half(u, 1), to_zm)

    def reduce1(u):
        for d, tag, to, lanes, step in ((0, "p", to_zp, high, 3), (1, "m", to_zm, low, -3)):
            arrived(f"z0{tag}", u, half(u, d))
            part = block(u, step, lanes)
            part[...] = part[...] + half(u, d)[...]
            send(f"z1{tag}", u, block(u, step), full(u, d, 0), to)

    def reduce_mid(u, i):
        for d, tag, to, step in ((0, "p", to_zp, 3 - i), (1, "m", to_zm, i - 3)):
            arrived(f"z{i}{tag}", u, full(u, d, i - 1))
            part = block(u, step)
            part[...] = part[...] + full(u, d, i - 1)[...]
            send(f"z{i + 1}{tag}", u, part, full(u, d, i), to)

    def final(u, c):
        q, j0, count = PARTS[u]
        return fin.at[j0:j0 + count, at(c * HALF + START[q], SIZES[q])]

    def reduce_end(u):
        q, j0, count = PARTS[u]
        arrived("z3p", u, full(u, 0, 2))
        arrived("z3m", u, full(u, 1, 2))
        total = (block(u, 0)[...] + (full(u, 0, 2)[...] + full(u, 1, 2)[...])) * SCALE
        first = core == 0
        final(u, core)[...] = jnp.where(first, total[..., low], total[..., high])
        away = fin_out.at[j0:j0 + count, START[q]:START[q] + SIZES[q]]
        away[...] = jnp.where(first, total[..., high], total[..., low])
        send("fin", u, away, final(u, core), sib)

    def exchange(kind, half):
        rows = at(core * UNIT + half * HALF, HALF)
        send(kind, None, raw.at[ylo, rows], raw.at[ylo, rows], sib)

    def means1():
        arrived("sib1", None, raw.at[ylo, at(other * UNIT + other * HALF, HALF)])
        msum[...] = jnp.zeros_like(msum)

        @pl.loop(0, 16)
        def _(i):
            part = raw[ylo, at(i * 64, 64), :]
            msum[0] = msum[0] + jnp.sum(part.reshape(8, 8, KU), axis=0)

        send("m1a", None, msum.at[0], m1.at[0], to_yb)
        send("m1b", None, msum.at[0], m1.at[1], to_yo)
        send("m1c", None, msum.at[0], m1.at[2], to_yd)

    def means2():
        for i, kind in enumerate(("m1a", "m1b", "m1c")):
            arrived(kind, None, m1.at[i])
        m2[0, ylo] = msum[0] + m1[2]
        m2[0, 1 - ylo] = m1[0] + m1[1]
        send("m2a", None, m2.at[0], m2.at[1], to_xp)
        send("m2b", None, m2.at[0], m2.at[2], to_xm)
        send("m2c", None, m2.at[0], m2.at[3], to_xd)

    @pl.loop(0, 8)
    def _(i):
        for s in range(2):
            raw[ylo, at(core * UNIT + i * 64, 64), s * PART:(s + 1) * PART] = in_ref[s, at(i * 64, 64), :]

    pl.semaphore_wait(barrier, len(peers))
    exchange("sib0", other)
    exchange("sib1", core)
    mine = core == ylo
    pl.when(mine)(early_own)
    pl.when(jnp.logical_not(mine))(early_away)
    arrived("sib0", None, raw.at[ylo, at(other * UNIT + core * HALF, HALF)])
    pl.when(mine)(early_away)
    pl.when(jnp.logical_not(mine))(early_own)
    for q in EARLY:
        sent.extend(own_copies(q) + (away("oa", q), away("ob", q)))

    steps = (
        lambda _: means1(), lambda _: means2(), send_rows, rows_ready,
        send_yb, send_yo, send_own, recv_next, pass_far, send_next, send_far, forward_own, forward_next, end_own,
        forward_far, across1, across2, columns, product, reduce0, reduce1,
        lambda u: reduce_mid(u, 1), lambda u: reduce_mid(u, 2), reduce_end,
    )
    done, marks = 0, []
    for step, index in ORDER:
        marks.append(len(sent))
        steps[step](index)
        if len(marks) > LAG:
            for c in sent[done:marks[-LAG]]:
                c.wait_send()
            done = marks[-LAG]
    for u in range(len(PARTS)):
        arrived("fin", u, final(u, other))
    for j in range(GROUPS):
        turned = fin[j].T
        for h in range(2):
            out_ref[h * HALF + j * GROUP:h * HALF + (j + 1) * GROUP, :] = turned[h * GROUP:(h + 1) * GROUP]
    for c in sent[done:]:
        c.wait_send()


def shards(log_derivs):
    f32, bf16, VMEM = jnp.float32, jnp.bfloat16, pltpu.VMEM
    rows, depth, width = 2 * UNIT, 2 * KU, 8 * max(SIZES)
    scratch = [
        VMEM((2, rows, KU), f32), VMEM((rows, depth), bf16), VMEM((rows, depth), bf16),
        VMEM((NX, 4 * HALF, KU), f32), VMEM((KEEP, width, depth), bf16), VMEM((KEEP, width, depth), bf16),
        VMEM((GROUPS, 8 * HALF, 4 * GROUP), f32),
        VMEM((2, GROUPS, HALF, 2 * GROUP), f32), VMEM((2, 3, GROUPS, HALF, 4 * GROUP), f32),
        VMEM((GROUPS, HALF, 2 * GROUP), f32), VMEM((GROUPS, UNIT, 2 * GROUP), f32),
        VMEM((1, 8, KU), f32), VMEM((3, 8, KU), f32), VMEM((4, 2, 8, KU), f32), VMEM((2, 1, KU), f32),
        pltpu.SemaphoreType.DMA((SEMS,)), pltpu.SemaphoreType.DMA((SEMS,)),
    ]
    return pl.pallas_call(
        kernel,
        out_shape=jax.ShapeDtypeStruct((UNIT, UNIT), f32),
        in_specs=[pl.BlockSpec(memory_space=VMEM)],
        out_specs=pl.BlockSpec(memory_space=VMEM),
        scratch_shapes=scratch,
        compiler_params=pltpu.CompilerParams(collective_id=0, has_side_effects=True, vmem_limit_bytes=60 * 2**20),
        cost_estimate=pl.CostEstimate(flops=20 * 10**9, bytes_accessed=4 * 2**20, transcendentals=0),
    )(log_derivs)


def solution(mesh):
    in_specs = (P(None, "samp", "par"),)
    out_specs = P("samp", "par")
    return jax.shard_map(shards, mesh=mesh, in_specs=in_specs, out_specs=out_specs, check_vma=False)
```

```python
import functools

import jax
import jax.numpy as jnp
from jax import lax
from jax.experimental import pallas as pl
from jax.experimental.pallas import tpu as pltpu
from jax.sharding import PartitionSpec as P

MESH = pl.DeviceIdType.MESH
NX, NY, NZ = 4, 4, 8
UNIT = 512
HALF = UNIT // 2
PART = 384
KEEP = 3
KU = 2 * PART
SIZES = (32, 32, 32, 32, 32, 32, 32, 32)
N = len(SIZES)
START = tuple(sum(SIZES[:q]) for q in range(N))
SAMPLES = 8192
SCALE = 1.0 / 12288.0
ACROSS = (False, False, True, True, True, True, True, True)
GROUP = 64
GROUPS = HALF // GROUP
EARLY = (0,)
PARTS = (
    (0, 0, 1), (0, 1, 1), (1, 0, 2), (0, 2, 1), (1, 2, 1), (0, 3, 1), (1, 3, 1), (2, 0, 4), (3, 0, 4), (4, 0, 4),
    (5, 0, 4), (6, 0, 4), (7, 0, 2), (7, 2, 2),
)

LAG = 70

ONCE = ["sib0", "sib1", "m1a", "m1b", "m1c", "m2a", "m2b", "m2c"] + [f"row{i}" for i in range(2 * GROUPS)]
EACH = [
    "oa", "ob", "j0", "g0", "xr0", "xl0", "fr0", "fl0", "xr1", "xl1", "fr1", "fl1", "xr2", "xl2", "fr2", "fl2",
]
REDUCE = ["z0p", "z0m", "z1p", "z1m", "z2p", "z2m", "z3p", "z3m", "fin"]
SEMS = len(ONCE) + N * len(EACH) + len(PARTS) * len(REDUCE)

ORDER = (
    (4, 0), (5, 0), (6, 0), (6, 2), (5, 1), (0, 0), (4, 1), (4, 2), (4, 3), (7, 0), (9, 0), (8, 0), (11, 2), (5, 3),
    (4, 4), (5, 5), (4, 5), (4, 6), (4, 7), (11, 0), (1, 0), (7, 1), (10, 0), (6, 1), (12, 0), (8, 1), (2, 0), (3,
    0), (13, 0), (8, 2), (5, 7), (14, 0), (10, 1), (9, 1), (7, 2), (7, 3), (5, 6), (13, 2), (5, 2), (5, 4), (11, 1),
    (15, 2), (16, 2), (6, 3), (8, 3), (2, 1), (3, 1), (14, 1), (7, 4), (17, 0), (18, 0), (18, 1), (19, 0), (7, 5),
    (19, 1), (12, 1), (8, 4), (8, 5), (2, 2), (3, 2), (20, 0), (6, 4), (9, 2), (20, 1), (13, 1), (17, 1), (18, 2),
    (19, 2), (11, 3), (15, 3), (18, 3), (19, 3), (18, 4), (19, 4), (7, 7), (21, 0), (20, 2), (7, 6), (9, 3), (8, 7),
    (8, 6), (2, 3), (3, 3), (18, 5), (19, 5), (21, 2), (13, 3), (16, 3), (12, 2), (20, 4), (20, 3), (9, 4), (18, 6),
    (19, 6), (20, 5), (21, 1), (11, 4), (22, 2), (10, 3), (15, 4), (22, 0), (21, 4), (10, 2), (12, 3), (21, 3), (20,
    6), (17, 2), (18, 7), (19, 7), (21, 5), (6, 5), (9, 5), (22, 1), (22, 4), (17, 3), (21, 6), (20, 7), (18, 8),
    (19, 8), (13, 4), (16, 4), (12, 4), (6, 6), (22, 5), (22, 3), (22, 6), (11, 5), (21, 7), (15, 5), (20, 8), (9,
    6), (10, 4), (17, 4), (18, 9), (19, 9), (11, 6), (13, 5), (16, 5), (22, 7), (23, 4), (10, 6), (12, 5), (6, 7),
    (23, 5), (20, 9), (13, 6), (16, 6), (21, 8), (23, 1), (23, 0), (9, 7), (10, 5), (17, 5), (15, 6), (11, 7), (15,
    7), (12, 6), (21, 9), (18, 10), (19, 10), (22, 8), (13, 7), (16, 7), (12, 7), (23, 6), (22, 9), (17, 6), (18,
    11), (19, 11), (20, 10), (10, 7), (17, 7), (18, 12), (19, 12), (20, 11), (21, 10), (20, 12), (23, 2), (18, 13),
    (19, 13), (23, 3), (21, 11), (21, 12), (20, 13), (23, 8), (23, 9), (22, 10), (21, 13), (22, 12), (22, 11), (22,
    13), (23, 7), (23, 12), (23, 10), (23, 11), (23, 13),
)


def slot(kind, q=None):
    if q is None:
        return ONCE.index(kind)
    if kind in REDUCE:
        return len(ONCE) + N * len(EACH) + q * len(REDUCE) + REDUCE.index(kind)
    return len(ONCE) + q * len(EACH) + EACH.index(kind)


def split(value):
    hi = value.astype(jnp.bfloat16)
    return hi, (value - hi.astype(jnp.float32)).astype(jnp.bfloat16)


def kernel(
    in_ref, out_ref,
    raw, rhi, rlo, cols, chi, clo, tile, zhalf, zfull, fin_out, fin,
    msum, m1, m2, mean, send_sem, recv_sem,
):
    samp, par = lax.axis_index("samp"), lax.axis_index("par")
    core, x, yhi = lax.rem(samp, 2), lax.rem(lax.div(samp, 2), NX), lax.div(samp, 2 * NX)
    z, ylo = lax.div(par, 2), lax.rem(par, 2)
    y = 2 * yhi + ylo
    other = 1 - core
    yb = y + 1 - 2 * ylo
    yo = lax.rem(y + 3 + 2 * ylo, NY)
    yd = lax.rem(y + 2, NY)
    xp, xm, xd = (lax.rem(x + d, NX) for d in (1, 3, 2))
    zp, zm = lax.rem(z + 1, NZ), lax.rem(z + NZ - 1, NZ)

    def dev(x=x, y=y, z=z, core=core):
        return (lax.div(y, 2) * (2 * NX) + x * 2 + core, z * 2 + lax.rem(y, 2))

    sib = dev(core=other)
    to_yb, to_yo, to_yd = dev(y=yb), dev(y=yo), dev(y=yd)
    to_xp, to_xm, to_xd = dev(x=xp), dev(x=xm), dev(x=xd)
    to_zp, to_zm = dev(z=zp), dev(z=zm)

    sent = []

    def copy(kind, q, src, dst, to):
        i = slot(kind, q)
        return pltpu.make_async_remote_copy(
            src_ref=src, dst_ref=dst, send_sem=send_sem.at[i], recv_sem=recv_sem.at[i], device_id=to, device_id_type=MESH
        )

    def send(kind, q, src, dst, to):
        go(copy(kind, q, src, dst, to))

    def go(c):
        c.start()
        sent.append(c)

    def arrived(kind, q, ref):
        copy(kind, q, ref, ref, sib).wait_recv()

    barrier = pltpu.get_barrier_semaphore()
    peers = (sib, to_yb, to_yo, to_yd, to_xp, to_xm, to_xd, to_zp, to_zm)
    for peer in peers:
        pl.semaphore_signal(barrier, inc=1, device_id=peer, device_id_type=MESH)

    def at(start, size):
        return pl.ds(pl.multiple_of(start, 8), size)

    def chunk_rows(colour, q):
        return at(colour * UNIT + core * HALF + START[q], SIZES[q])

    def piece(x, rel, q, size=1):
        return cols.at[x, at(4 * START[q] + rel * SIZES[q], size * SIZES[q])]

    def away(kind, q):
        src = raw.at[ylo, chunk_rows(1 - ylo, q)]
        if kind == "oa":
            return copy(kind, q, src, piece(x, ylo, q), to_yb)
        return copy(kind, q, src, piece(x, 1 - ylo, q), to_yo)

    def send_yo(q):
        if q not in EARLY:
            go(away("ob", q))

    def send_yb(q):
        if q not in EARLY:
            go(away("oa", q))
        rows = raw.at[ylo, chunk_rows(ylo, q)]
        send("j0", q, rows, rows, to_yb)

    def own_copies(q):
        own = piece(x, 2, q)
        return copy("xr0", q, own, own, to_xp), copy("xl0", q, own, own, to_xm)

    def place_own(q):
        own = piece(x, 2, q)
        own[...] = raw[ylo, chunk_rows(ylo, q), :]

    def send_own(q):
        if q not in EARLY:
            place_own(q)
            for c in own_copies(q):
                go(c)

    def early_own():
        for q in EARLY:
            place_own(q)
            for c in own_copies(q):
                c.start()

    def early_away():
        for q in EARLY:
            away("oa", q).start()
            away("ob", q).start()

    def recv_next(q):
        arrived("oa", q, piece(x, 1 - ylo, q))
        raw[1 - ylo, chunk_rows(ylo, q), :] = piece(x, 1 - ylo, q)[...]

    def send_next(q):
        arrived("ob", q, piece(x, ylo, q))
        both = piece(x, 0, q, 2)
        send("xr1", q, both, both, to_xp)
        send("xl1", q, both, both, to_xm)

    def pass_far(q):
        passed = raw.at[1 - ylo, chunk_rows(1 - ylo, q)]
        arrived("j0", q, passed)
        send("g0", q, passed, piece(x, 3, q), to_yo)

    def send_far(q):
        arrived("g0", q, piece(x, 3, q))
        if not ACROSS[q]:
            far = piece(x, 3, q)
            send("xr2", q, far, far, to_xp)
            send("xl2", q, far, far, to_xm)

    def halves(rel, x, q):
        h = SIZES[q] // 2
        first = 4 * START[q] + rel * SIZES[q]
        return cols.at[x, at(first, h)], cols.at[x, at(first + h, h)]

    def forward_one(i, rel, q):
        arrived(f"xr{i}", q, piece(xm, rel, q))
        low = halves(rel, xm, q)[0]
        send(f"fr{i}", q, low, low, to_xp)
        arrived(f"xl{i}", q, piece(xp, rel, q))
        high = halves(rel, xp, q)[1]
        send(f"fl{i}", q, high, high, to_xm)

    def end_one(i, rel, q):
        low, high = halves(rel, xd, q)
        arrived(f"fr{i}", q, low)
        arrived(f"fl{i}", q, high)

    def forward_own(q):
        forward_one(0, 2, q)

    def across1(q):
        send("xr2", q, piece(xm, 2, q), piece(xm, 3, q), to_yd)
        send("xl2", q, piece(xp, 2, q), piece(xp, 3, q), to_yd)

    def across2(q):
        send("fr2", q, piece(xd, 2, q), piece(xd, 3, q), to_yd)

    def end_own(q):
        end_one(0, 2, q)

    def forward_next(q):
        arrived("xr1", q, piece(xm, 0, q, 2))
        low = piece(xm, 0, q)
        send("fr1", q, low, low, to_xp)
        arrived("xl1", q, piece(xp, 0, q, 2))
        high = piece(xp, 1, q)
        send("fl1", q, high, high, to_xm)

    def forward_far(q):
        forward_one(2, 3, q)

    def columns_ready(q):
        arrived("fr1", q, piece(xd, 0, q))
        arrived("fl1", q, piece(xd, 1, q))
        if ACROSS[q]:
            arrived("xr2", q, piece(xm, 3, q))
            arrived("xl2", q, piece(xp, 3, q))
            arrived("fr2", q, piece(xd, 3, q))
        else:
            end_one(2, 3, q)

    def send_rows(j):
        for c in range(2):
            rows = at(c * UNIT + core * HALF + j * GROUP, GROUP)
            send(f"row{2 * j + c}", None, raw.at[1 - ylo, rows], raw.at[1 - ylo, rows], sib)

    def rows_ready(j):
        if j == 0:
            for i, kind in enumerate(("m2a", "m2b", "m2c")):
                arrived(kind, None, m2.at[i + 1])
            total = (m2[0] + m2[1]) + (m2[2] + m2[3])
            mean[...] = jnp.sum(total, axis=1, keepdims=True) / SAMPLES
        for c in range(2):
            arrived(f"row{2 * j + c}", None, raw.at[1 - ylo, at(c * UNIT + other * HALF + j * GROUP, GROUP)])

        @pl.loop(0, GROUP // 16)
        def _(i):
            n = GROUP // 64
            src = at(lax.div(i, n) * HALF + j * GROUP + lax.rem(i, n) * 64, 64)
            dst = at(j * 4 * GROUP + i * 64, 64)
            for p in range(2):
                hi, lo = split(raw[p, src, :] - mean[p])
                rhi[dst, p * KU:(p + 1) * KU] = hi
                rlo[dst, p * KU:(p + 1) * KU] = lo

    def columns(q):
        columns_ready(q)
        keep, size = q % KEEP, SIZES[q]

        @pl.loop(0, 8)
        def _(s):
            to = pl.ds(pl.multiple_of(s * size, 16), size)
            for p in range(2):
                off = lax.rem(2 * lax.div(s, NX) + p - y + NY, NY)
                rel = jnp.where(off == 0, 2, jnp.where(off == 1, 1, jnp.where(off == 2, 3, 0)))
                hi, lo = split(piece(lax.rem(s, NX), rel, q)[...] - mean[p])
                chi[keep, to, p * KU:(p + 1) * KU] = hi
                clo[keep, to, p * KU:(p + 1) * KU] = lo

    dims = (((1,), (1,)), ((), ()))
    dot = functools.partial(lax.dot_general, dimension_numbers=dims, preferred_element_type=jnp.float32)

    def product(u):
        q, j0, count = PARTS[u]
        keep, width = q % KEEP, 8 * SIZES[q]

        def some(r):
            rows = pl.ds(pl.multiple_of(j0 * 4 * GROUP + r * HALF, HALF), HALF)
            n = GROUP // 64
            lanes = pl.ds(pl.multiple_of(lax.rem(r, n) * HALF, HALF), HALF)
            ch, rh = chi[keep, :width], rhi[rows, :]
            tile[j0 + lax.div(r, n), 8 * START[q]:8 * START[q] + width, lanes] = (
                dot(ch, rh) + dot(ch, rlo[rows, :]) + dot(clo[keep, :width], rh)
            )

        if count == 4:
            pl.loop(0, 2)(lambda r: (some(2 * r), some(2 * r + 1)) and None)
        else:
            pl.loop(0, count * GROUP // 64)(some)

    def block(u, step, lanes=slice(None)):
        q, j0, count = PARTS[u]
        rows = at(8 * START[q] + lax.rem(z + step + NZ, NZ) * SIZES[q], SIZES[q])
        return tile.at[j0:j0 + count, rows, lanes]

    def full(u, d, i):
        q, j0, count = PARTS[u]
        return zfull.at[d, i, j0:j0 + count, START[q]:START[q] + SIZES[q]]

    def half(u, d):
        q, j0, count = PARTS[u]
        return zhalf.at[d, j0:j0 + count, START[q]:START[q] + SIZES[q]]

    low, high = slice(0, 2 * GROUP), slice(2 * GROUP, 4 * GROUP)

    def reduce0(u):
        send("z0p", u, block(u, 4, high), half(u, 0), to_zp)
        send("z0m", u, block(u, 4, low), half(u, 1), to_zm)

    def reduce1(u):
        for d, tag, to, lanes, step in ((0, "p", to_zp, high, 3), (1, "m", to_zm, low, -3)):
            arrived(f"z0{tag}", u, half(u, d))
            part = block(u, step, lanes)
            part[...] = part[...] + half(u, d)[...]
            send(f"z1{tag}", u, block(u, step), full(u, d, 0), to)

    def reduce_mid(u, i):
        for d, tag, to, step in ((0, "p", to_zp, 3 - i), (1, "m", to_zm, i - 3)):
            arrived(f"z{i}{tag}", u, full(u, d, i - 1))
            part = block(u, step)
            part[...] = part[...] + full(u, d, i - 1)[...]
            send(f"z{i + 1}{tag}", u, part, full(u, d, i), to)

    def final(u, c):
        q, j0, count = PARTS[u]
        return fin.at[j0:j0 + count, at(c * HALF + START[q], SIZES[q])]

    def reduce_end(u):
        q, j0, count = PARTS[u]
        arrived("z3p", u, full(u, 0, 2))
        arrived("z3m", u, full(u, 1, 2))
        total = (block(u, 0)[...] + (full(u, 0, 2)[...] + full(u, 1, 2)[...])) * SCALE
        first = core == 0
        final(u, core)[...] = jnp.where(first, total[..., low], total[..., high])
        away = fin_out.at[j0:j0 + count, START[q]:START[q] + SIZES[q]]
        away[...] = jnp.where(first, total[..., high], total[..., low])
        send("fin", u, away, final(u, core), sib)

    def exchange(kind, half):
        rows = at(core * UNIT + half * HALF, HALF)
        send(kind, None, raw.at[ylo, rows], raw.at[ylo, rows], sib)

    def means1():
        arrived("sib1", None, raw.at[ylo, at(other * UNIT + other * HALF, HALF)])
        msum[...] = jnp.zeros_like(msum)

        @pl.loop(0, 16)
        def _(i):
            part = raw[ylo, at(i * 64, 64), :]
            msum[0] = msum[0] + jnp.sum(part.reshape(8, 8, KU), axis=0)

        send("m1a", None, msum.at[0], m1.at[0], to_yb)
        send("m1b", None, msum.at[0], m1.at[1], to_yo)
        send("m1c", None, msum.at[0], m1.at[2], to_yd)

    def means2():
        for i, kind in enumerate(("m1a", "m1b", "m1c")):
            arrived(kind, None, m1.at[i])
        m2[0, ylo] = msum[0] + m1[2]
        m2[0, 1 - ylo] = m1[0] + m1[1]
        send("m2a", None, m2.at[0], m2.at[1], to_xp)
        send("m2b", None, m2.at[0], m2.at[2], to_xm)
        send("m2c", None, m2.at[0], m2.at[3], to_xd)

    @pl.loop(0, 8)
    def _(i):
        for s in range(2):
            raw[ylo, at(core * UNIT + i * 64, 64), s * PART:(s + 1) * PART] = in_ref[s, at(i * 64, 64), :]

    pl.semaphore_wait(barrier, len(peers))
    exchange("sib0", other)
    exchange("sib1", core)
    mine = core == ylo
    pl.when(mine)(early_own)
    pl.when(jnp.logical_not(mine))(early_away)
    arrived("sib0", None, raw.at[ylo, at(other * UNIT + core * HALF, HALF)])
    pl.when(mine)(early_away)
    pl.when(jnp.logical_not(mine))(early_own)
    for q in EARLY:
        sent.extend(own_copies(q) + (away("oa", q), away("ob", q)))

    steps = (
        lambda _: means1(), lambda _: means2(), send_rows, rows_ready,
        send_yb, send_yo, send_own, recv_next, pass_far, send_next, send_far, forward_own, forward_next, end_own,
        forward_far, across1, across2, columns, product, reduce0, reduce1,
        lambda u: reduce_mid(u, 1), lambda u: reduce_mid(u, 2), reduce_end,
    )
    done, marks = 0, []
    for step, index in ORDER:
        marks.append(len(sent))
        steps[step](index)
        if len(marks) > LAG:
            for c in sent[done:marks[-LAG]]:
                c.wait_send()
            done = marks[-LAG]
    for u in range(len(PARTS)):
        arrived("fin", u, final(u, other))
    for j in range(GROUPS):
        turned = fin[j].T
        for h in range(2):
            out_ref[h * HALF + j * GROUP:h * HALF + (j + 1) * GROUP, :] = turned[h * GROUP:(h + 1) * GROUP]
    for c in sent[done:]:
        c.wait_send()


def shards(log_derivs):
    f32, bf16, VMEM = jnp.float32, jnp.bfloat16, pltpu.VMEM
    rows, depth, width = 2 * UNIT, 2 * KU, 8 * max(SIZES)
    scratch = [
        VMEM((2, rows, KU), f32), VMEM((rows, depth), bf16), VMEM((rows, depth), bf16),
        VMEM((NX, 4 * HALF, KU), f32), VMEM((KEEP, width, depth), bf16), VMEM((KEEP, width, depth), bf16),
        VMEM((GROUPS, 8 * HALF, 4 * GROUP), f32),
        VMEM((2, GROUPS, HALF, 2 * GROUP), f32), VMEM((2, 3, GROUPS, HALF, 4 * GROUP), f32),
        VMEM((GROUPS, HALF, 2 * GROUP), f32), VMEM((GROUPS, UNIT, 2 * GROUP), f32),
        VMEM((1, 8, KU), f32), VMEM((3, 8, KU), f32), VMEM((4, 2, 8, KU), f32), VMEM((2, 1, KU), f32),
        pltpu.SemaphoreType.DMA((SEMS,)), pltpu.SemaphoreType.DMA((SEMS,)),
    ]
    return pl.pallas_call(
        kernel,
        out_shape=jax.ShapeDtypeStruct((UNIT, UNIT), f32),
        in_specs=[pl.BlockSpec(memory_space=VMEM)],
        out_specs=pl.BlockSpec(memory_space=VMEM),
        scratch_shapes=scratch,
        compiler_params=pltpu.CompilerParams(collective_id=0, has_side_effects=True, vmem_limit_bytes=60 * 2**20),
        cost_estimate=pl.CostEstimate(flops=20 * 10**9, bytes_accessed=4 * 2**20, transcendentals=0),
    )(log_derivs)


def solution(mesh):
    in_specs = (P(None, "samp", "par"),)
    out_specs = P("samp", "par")
    return jax.shard_map(shards, mesh=mesh, in_specs=in_specs, out_specs=out_specs, check_vma=False)
```
